32 devices in a mesh: blk: 4 (over x, core), eng: 8 (over z, y).
Axes of the slice: x: 2, y: 2, z: 4, core: 2. Of those that a mesh axis runs over, the one named last changes fastest.
Arguments:
- g_lesser: bfloat16 [32, 4, 2, 256, 256], P('eng', 'blk'), may hold values from -6 to 6
- g_greater: bfloat16 [32, 4, 2, 256, 256], P('eng', 'blk'), may hold values from -6 to 6
- coulomb: bfloat16 [4, 2, 256, 256], P('blk'), may hold values from -0.21875 to 0.21875
- coupling: int32 [4], P('blk'), may hold values 0 or 1
- lag_slots: int32 [32], replicated, may hold values from 0 to 31
Outputs:
- sigma_lesser: bfloat16 [32, 4, 2, 256, 256], P('eng', 'blk')
- sigma_greater: bfloat16 [32, 4, 2, 256, 256], P('eng', 'blk')
The draws below stay inside these ranges and needn't reach their ends.
Inputs may be any that keep to these rules, and one draw needn't show every extreme that they name: `lag_slots`: offsets may repeat across slots.
All inputs are finite; a program needn't handle non-finite values. No bound on the sum of `coupling` on one device may be relied on, other than what follows from the above.
Results may differ from the reference program's by a relative error of at most 0.0065.
Values may be sent and summed in bfloat16 or wider, within the bound.
A program may use at most 128 MiB of HBM per device.

```python
import jax
import jax.numpy as jnp
from jax import lax

BS = 256
NB = 4
NE = 32


def touch_ends(result, rng, least, top_value):
    longest = result.shape.index(max(result.shape))
    spots = []
    for shift in (0, 1):
        where = [jax.random.randint(jax.random.fold_in(rng, axis), (), 0, length) for axis, length in enumerate(result.shape)]
        where[longest] = (where[longest] + shift) % result.shape[longest]
        spots.append(tuple(where))
    return result.at[spots[0]].set(least).at[spots[1]].set(top_value)


def levels(own_key, shape, pieces, smallest, largest):
    gain, own = 1.0, jax.random.fold_in(own_key, 6)
    for position, shards_of in pieces:
        steps = jnp.exp(jax.random.uniform(jax.random.fold_in(own, position), (shards_of,), jnp.float32, smallest / len(pieces), largest / len(pieces)))
        gain = gain * jnp.repeat(steps, shape[position] // shards_of).reshape([-1 if axis == position else 1 for axis in range(len(shape))])
    return gain


def bell_draw(rng, shape, spread, bound, pieces=(), held_as=jnp.bfloat16):
    factor_of = levels(rng, shape, pieces, -0.22, 0.18) if pieces else 1.0
    entries = jax.random.normal(rng, shape, jnp.float32) * spread * factor_of
    return jnp.minimum(jnp.maximum(entries, -bound), bound).astype(held_as)


def setup_inputs(seed: int = 0) -> dict:
    splits = jax.random.split(jax.random.key(seed), 6)
    g_lesser = bell_draw(splits[0], (NE, NB, 2, BS, BS), 1.0, 6.0, ((0, 8), (1, 4)))
    g_greater = bell_draw(splits[1], (NE, NB, 2, BS, BS), 1.0, 6.0, ((0, 8), (1, 4)))
    coulomb = bell_draw(splits[2], (NB, 2, BS, BS), (3 * BS) ** -0.5, 0.21875, ((0, 4),))
    coupling = touch_ends((jax.random.randint(splits[3], (NB,), 0, 4) < 3).astype(jnp.int32), jax.random.fold_in(splits[3], 1), 0, 1)
    lag_slots = touch_ends(jax.random.randint(splits[4], (NE,), 0, NE), jax.random.fold_in(splits[4], 1), 0, NE - 1).astype(jnp.int32)
    return dict(g_lesser=g_lesser, g_greater=g_greater, coulomb=coulomb, coupling=coupling, lag_slots=lag_slots)


def product(einsum_form, left_side, right_side):
    return jnp.einsum(einsum_form, left_side.astype(jnp.float32), right_side.astype(jnp.float32), precision=lax.Precision.HIGHEST)


def screen(pad_p, pad_v):
    row_count = pad_v.shape[0] - 2
    v_diag_zero = pad_v[1:row_count + 1, 0]
    v_diag_plus = pad_v[2:, 0]
    v_up_minus = pad_v[:row_count, 1]
    v_up_zero = pad_v[1:row_count + 1, 1]
    v_up_plus = pad_v[2:, 1]
    p_diag_minus = pad_p[:, :row_count, 0]
    p_diag_zero = pad_p[:, 1:row_count + 1, 0]
    p_diag_plus = pad_p[:, 2:, 0]
    p_up_minus = pad_p[:, :row_count, 1]
    p_up_zero = pad_p[:, 1:row_count + 1, 1]
    p_up_plus = pad_p[:, 2:, 1]
    q_minus = (product("rba,krbc->krac", v_up_minus, p_diag_minus) + product("rab,krcb->krac", v_diag_zero, p_up_minus)).astype(jnp.bfloat16)
    q_zero = (product("rba,krbc->krac", v_up_minus, p_up_minus) + product("rab,krbc->krac", v_diag_zero, p_diag_zero) + product("rab,krcb->krac", v_up_zero, p_up_zero)).astype(jnp.bfloat16)
    q_plus = (product("rab,krbc->krac", v_diag_zero, p_up_zero) + product("rab,krbc->krac", v_up_zero, p_diag_plus)).astype(jnp.bfloat16)
    q_far = product("rab,krbc->krac", v_up_zero, p_up_plus).astype(jnp.bfloat16)
    w_diag = product("krab,rbc->krac", q_minus, v_up_minus) + product("krab,rbc->krac", q_zero, v_diag_zero) + product("krab,rcb->krac", q_plus, v_up_zero)
    w_upper = product("krab,rbc->krac", q_zero, v_up_zero) + product("krab,rbc->krac", q_plus, v_diag_plus) + product("krab,rcb->krac", q_far, v_up_plus)
    return jnp.stack([w_diag, w_upper], axis=2).astype(jnp.bfloat16)


def reference(g_lesser, g_greater, coulomb, coupling, lag_slots):
    norm_factor = NE ** -0.5

    def polar_row(kind_pair):
        lesser = kind_pair[0].astype(jnp.float32)
        greater = kind_pair[1].astype(jnp.float32)
        f_lesser = jnp.fft.rfft(lesser, axis=0)
        f_greater = jnp.fft.rfft(greater, axis=0)
        c_lesser = jnp.fft.irfft(f_lesser * jnp.conj(f_greater), n=NE, axis=0)
        c_greater = jnp.fft.irfft(f_greater * jnp.conj(f_lesser), n=NE, axis=0)
        return ((c_lesser[lag_slots] * norm_factor).astype(jnp.bfloat16), (c_greater[lag_slots] * norm_factor).astype(jnp.bfloat16))

    by_rows = (jnp.moveaxis(g_lesser, 1, 0), jnp.moveaxis(g_greater, 1, 0))
    p_lesser, p_greater = lax.map(polar_row, by_rows)
    polarization = jnp.stack([jnp.moveaxis(p_lesser, 0, 1), jnp.moveaxis(p_greater, 0, 1)], axis=1)

    row_ids = jnp.arange(NB, dtype=jnp.int32)
    kept_links = (coupling * (row_ids < NB - 1).astype(jnp.int32)).astype(jnp.bfloat16)
    v_both = jnp.stack([coulomb[:, 0], coulomb[:, 1] * kept_links[:, None, None]], axis=1)
    pad_v = jnp.pad(v_both, ((1, 1), (0, 0), (0, 0), (0, 0)))

    def screen_energy(kind_pair):
        return screen(jnp.pad(kind_pair, ((0, 0), (1, 1), (0, 0), (0, 0), (0, 0))), pad_v)

    screened = lax.map(screen_energy, polarization)
    w_rows_lesser = jnp.moveaxis(screened[:, 0], 1, 0)
    w_rows_greater = jnp.moveaxis(screened[:, 1], 1, 0)

    def convolve_kind(green_part, screened_part):
        placed = jnp.zeros(screened_part.shape, jnp.float32).at[lag_slots].add(screened_part.astype(jnp.float32))
        spectrum = jnp.fft.rfft(green_part.astype(jnp.float32), axis=0) * jnp.fft.rfft(placed, axis=0)
        return (jnp.fft.irfft(spectrum, n=NE, axis=0) * norm_factor).astype(jnp.bfloat16)

    def self_row(row_data):
        return (convolve_kind(row_data[0], row_data[2]), convolve_kind(row_data[1], row_data[3]))

    s_lesser, s_greater = lax.map(self_row, (by_rows[0], by_rows[1], w_rows_lesser, w_rows_greater))
    return (jnp.moveaxis(s_lesser, 0, 1), jnp.moveaxis(s_greater, 0, 1))
```

```python
import math

import jax
import jax.numpy as jnp
from jax import lax
from jax.sharding import PartitionSpec as P


def padded_2(array, sides, width):
    for axis, dim in sides:
        devices, length = (lax.axis_size(axis), array.shape[dim])
        up = [(i, (i + 1) % devices) for i in range(devices - 1)]
        down = [(j, i) for i, j in up]
        last = lax.slice_in_dim(array, length - width, length, axis=dim)
        leading = lax.slice_in_dim(array, 0, width, axis=dim)
        before = lax.ppermute(last, axis, up)
        after = lax.ppermute(leading, axis, down)
        array = jnp.concatenate([before, array, after], axis=dim)
    return array


def product(einsum_form, left_side, right_side):
    return jnp.einsum(einsum_form, left_side, right_side, preferred_element_type=jnp.float32)


def screen(pad_p, pad_v):
    row_count = pad_v.shape[0] - 2
    v_diag_zero = pad_v[1 : row_count + 1, 0]
    v_diag_plus = pad_v[2:, 0]
    v_up_minus = pad_v[:row_count, 1]
    v_up_zero = pad_v[1 : row_count + 1, 1]
    v_up_plus = pad_v[2:, 1]
    p_diag_minus = pad_p[:, :row_count, 0]
    p_diag_zero = pad_p[:, 1 : row_count + 1, 0]
    p_diag_plus = pad_p[:, 2:, 0]
    p_up_minus = pad_p[:, :row_count, 1]
    p_up_zero = pad_p[:, 1 : row_count + 1, 1]
    p_up_plus = pad_p[:, 2:, 1]
    q_minus = (
        product("rba,krbc->krac", v_up_minus, p_diag_minus)
        + product("rab,krcb->krac", v_diag_zero, p_up_minus)
    ).astype(jnp.bfloat16)
    q_zero = (
        product("rba,krbc->krac", v_up_minus, p_up_minus)
        + product("rab,krbc->krac", v_diag_zero, p_diag_zero)
        + product("rab,krcb->krac", v_up_zero, p_up_zero)
    ).astype(jnp.bfloat16)
    q_plus = (
        product("rab,krbc->krac", v_diag_zero, p_up_zero)
        + product("rab,krbc->krac", v_up_zero, p_diag_plus)
    ).astype(jnp.bfloat16)
    q_far = product("rab,krbc->krac", v_up_zero, p_up_plus).astype(jnp.bfloat16)
    w_diag = (
        product("krab,rbc->krac", q_minus, v_up_minus)
        + product("krab,rbc->krac", q_zero, v_diag_zero)
        + product("krab,rcb->krac", q_plus, v_up_zero)
    )
    w_upper = (
        product("krab,rbc->krac", q_zero, v_up_zero)
        + product("krab,rbc->krac", q_plus, v_diag_plus)
        + product("krab,rcb->krac", q_far, v_up_plus)
    )
    return jnp.stack([w_diag, w_upper], axis=2).astype(jnp.bfloat16)


def tables(row_ids, column_ids, energies):
    phase_ids = row_ids[:, None] * column_ids[None, :] % energies
    angles = phase_ids.astype(jnp.float32) * (2.0 * math.pi / energies)
    return (jnp.cos(angles), jnp.sin(angles))


def matmul(lookup_table, values_in):
    return jnp.dot(
        lookup_table, values_in, precision=lax.Precision.HIGHEST, preferred_element_type=jnp.float32
    )


def correlate(lesser, greater):
    energies = lesser.shape[0]
    layout = lesser.shape
    slot_ids = jnp.arange(energies, dtype=jnp.int32)
    cos_tab, sin_tab = tables(slot_ids, slot_ids, energies)
    flat_lesser = lesser.reshape(energies, -1).astype(jnp.float32)
    flat_greater = greater.reshape(energies, -1).astype(jnp.float32)
    lesser_re = matmul(cos_tab, flat_lesser)
    lesser_im = -matmul(sin_tab, flat_lesser)
    greater_re = matmul(cos_tab, flat_greater)
    greater_im = -matmul(sin_tab, flat_greater)
    cross_re = lesser_re * greater_re + lesser_im * greater_im
    cross_im = lesser_im * greater_re - lesser_re * greater_im
    back = matmul(cos_tab, cross_re) - matmul(sin_tab, cross_im)
    return (back * (energies ** (-1.5))).astype(jnp.bfloat16).reshape(layout)


def convolve_pair(green_lesser, green_greater, screened, lag_slots):
    energies = green_lesser.shape[0]
    layout = green_lesser.shape
    slot_ids = jnp.arange(energies, dtype=jnp.int32)
    cos_tab, sin_tab = tables(slot_ids, slot_ids, energies)
    hits = jnp.sum((lag_slots[:, None] == slot_ids[None, :]).astype(jnp.float32), axis=0)
    mirrored = jnp.roll(hits[::-1], 1)
    flat_screen = screened.reshape(energies, -1).astype(jnp.float32)

    def convolve_kind(green_part, weights, sign):
        flat_green = green_part.reshape(energies, -1).astype(jnp.float32)
        green_re = matmul(cos_tab, flat_green)
        green_im = -matmul(sin_tab, flat_green)
        screen_re = matmul(cos_tab * weights[None, :], flat_screen)
        screen_im = -sign * matmul(sin_tab * weights[None, :], flat_screen)
        joint_re = green_re * screen_re - green_im * screen_im
        joint_im = green_re * screen_im + green_im * screen_re
        result = matmul(cos_tab, joint_re) - matmul(sin_tab, joint_im)
        return (result * (energies ** (-1.5))).astype(jnp.bfloat16).reshape(layout)

    return (convolve_kind(green_lesser, hits, 1.0), convolve_kind(green_greater, mirrored, -1.0))


def on_device(g_lesser, g_greater, coulomb, coupling, lag_slots):
    own_energies = g_lesser.shape[0]
    row_count = g_lesser.shape[1]
    el_lesser, el_greater = (
        lax.all_to_all(g_lesser, "eng", split_axis=3, concat_axis=0, tiled=True),
        lax.all_to_all(g_greater, "eng", split_axis=3, concat_axis=0, tiled=True),
    )
    polar = correlate(el_lesser, el_greater)
    polar = lax.all_to_all(polar, "eng", split_axis=0, concat_axis=3, tiled=True)
    row_ids = lax.axis_index("blk") * row_count + jnp.arange(row_count, dtype=jnp.int32)
    all_rows = row_count * lax.axis_size("blk")
    kept_links = (coupling * (row_ids < all_rows - 1).astype(jnp.int32)).astype(jnp.bfloat16)
    v_both = jnp.stack([coulomb[:, 0], coulomb[:, 1] * kept_links[:, None, None]], axis=1)
    pad_v = padded_2(v_both[None], (("blk", 1),), 1)[0]
    pad_p = padded_2(polar, (("blk", 1),), 1)
    screened = screen(pad_p, pad_v)
    w_el = lax.all_to_all(screened, "eng", split_axis=3, concat_axis=0, tiled=True)
    self_lesser, self_greater = convolve_pair(el_lesser, el_greater, w_el, lag_slots)
    sigma_lesser, sigma_greater = (
        lax.all_to_all(self_lesser, "eng", split_axis=0, concat_axis=3, tiled=True),
        lax.all_to_all(self_greater, "eng", split_axis=0, concat_axis=3, tiled=True),
    )
    return (sigma_lesser, sigma_greater)


def solution(mesh):
    return jax.shard_map(
        on_device,
        mesh=mesh,
        in_specs=(
            P("eng", "blk", None, None, None),
            P("eng", "blk", None, None, None),
            P("blk", None, None, None),
            P("blk"),
            P(),
        ),
        out_specs=(P("eng", "blk", None, None, None), P("eng", "blk", None, None, None)),
        check_vma=False,
    )
```

```python
import functools

import jax
import jax.numpy as jnp
from jax import lax
from jax.experimental import pallas as pl
from jax.experimental.pallas import tpu as pltpu
from jax.sharding import PartitionSpec as P

MESH = pl.DeviceIdType.MESH
LANES = 128
PACK = 16
DIRECT = 8


def correlate(first, second, sign=1.0):
    count = first.shape[0]
    if sign > 0 and count > DIRECT and count % 2 == 0:
        half = count // 2
        first_lo, first_hi = first[:half], first[half:]
        second_lo, second_hi = second[:half] * 0.5, second[half:] * 0.5
        even = correlate(first_lo + first_hi, second_lo + second_hi)
        odd = correlate(first_lo - first_hi, second_lo - second_hi, -1.0)
        return jnp.concatenate([even + odd, even - odd], axis=0)
    wrapped = jnp.concatenate([first, first if sign > 0 else -first], axis=0)
    total = second[0:1] * wrapped[:count]
    for j in range(1, count):
        total = total + second[j : j + 1] * wrapped[j : j + count]
    return total


def convolve(first, second, sign=1.0):
    count = first.shape[0]
    if sign > 0 and count > DIRECT and count % 2 == 0:
        half = count // 2
        first_lo, first_hi = first[:half], first[half:]
        second_lo, second_hi = second[:half] * 0.5, second[half:] * 0.5
        even = convolve(first_lo + first_hi, second_lo + second_hi)
        odd = convolve(first_lo - first_hi, second_lo - second_hi, -1.0)
        return jnp.concatenate([even + odd, even - odd], axis=0)
    wrapped = jnp.concatenate([first if sign > 0 else -first, first], axis=0)
    total = second[0:1] * wrapped[count:]
    for j in range(1, count):
        total = total + second[j : j + 1] * wrapped[count - j : 2 * count - j]
    return total


def dot(left, right):
    return jnp.dot(left, right, preferred_element_type=jnp.float32)


def dot_t(left, right):
    return lax.dot_general(
        left, right, (((1,), (1,)), ((), ())), preferred_element_type=jnp.float32
    )


def kernel(
    n_blk,
    n_eng,
    gl_ref,
    gg_ref,
    v_ref,
    weight_ref,
    sl_ref,
    sg_ref,
    green,
    polar_el,
    polar,
    v_all,
    w_own,
    w_el,
    sigma,
    g_send,
    g_recv,
    p_send,
    p_recv,
    halo_send,
    halo_recv,
    v_send,
    v_recv,
    w_send,
    w_recv,
    s_send,
    s_recv,
    local_g,
    local_p,
    local_w,
    local_s,
    local_v,
):
    blk = lax.axis_index("blk")
    me = lax.axis_index("eng")
    own, blocks, size = gl_ref.shape[0], gl_ref.shape[2], gl_ref.shape[3]
    energies = own * n_eng
    rows = size // n_eng
    scale = energies ** (-0.5)
    has_left, has_right = blk > 0, blk < n_blk - 1
    g_refs, s_refs = (gl_ref, gg_ref), (sl_ref, sg_ref)

    def peer_of(step):
        return lax.rem(me + step, n_eng)

    def part(index, length):
        return pl.ds(pl.multiple_of(index * length, length), length)

    def remote(src, dst, send, recv, blk_to, eng_to):
        return pltpu.make_async_remote_copy(
            src_ref=src,
            dst_ref=dst,
            send_sem=send,
            recv_sem=recv,
            device_id=(blk_to, eng_to),
            device_id_type=MESH,
        )

    def each(body, low=1, high=n_eng):
        def run(step, carry):
            body(step)
            return carry

        lax.fori_loop(low, high, run, 0)

    def g_copy(kind, b, step):
        return remote(
            g_refs[kind].at[:, 0, b, part(peer_of(step), rows), :],
            green.at[kind, part(me, own), b],
            g_send.at[kind, b, step],
            g_recv.at[kind, b, step],
            blk,
            peer_of(step),
        )

    def g_local(kind, b):
        return pltpu.make_async_copy(
            g_refs[kind].at[:, 0, b, part(me, rows), :],
            green.at[kind, part(me, own), b],
            local_g.at[kind, b],
        )

    def p_copy(slot, b, step):
        return remote(
            polar_el.at[peer_of(step) * own + slot, b],
            polar.at[1, slot, b, part(me, rows), :],
            p_send.at[slot, b, step],
            p_recv.at[slot, b, step],
            blk,
            peer_of(step),
        )

    def p_local(slot, b):
        return pltpu.make_async_copy(
            polar_el.at[me * own + slot, b],
            polar.at[1, slot, b, part(me, rows), :],
            local_p.at[slot, b],
        )

    def halo_copy(slot, side):
        return remote(
            polar.at[1, slot],
            polar.at[2 - 2 * side, slot],
            halo_send.at[slot, side],
            halo_recv.at[slot, side],
            lax.rem(blk - 1 + 2 * side + n_blk, n_blk),
            me,
        )

    def v_copy(side):
        return remote(
            v_ref,
            v_all.at[2 - 2 * side],
            v_send.at[side],
            v_recv.at[side],
            lax.rem(blk - 1 + 2 * side + n_blk, n_blk),
            me,
        )

    def w_copy(slot, step):
        return remote(
            w_own.at[slot, :, part(peer_of(step), rows), :],
            w_el.at[me * own + slot],
            w_send.at[slot, step],
            w_recv.at[slot, step],
            blk,
            peer_of(step),
        )

    def w_local(slot):
        return pltpu.make_async_copy(
            w_own.at[slot, :, part(me, rows), :], w_el.at[me * own + slot], local_w.at[slot]
        )

    def s_copy(kind, b, step):
        return remote(
            sigma.at[kind, part(peer_of(step), own), b],
            s_refs[kind].at[:, 0, b, part(me, rows), :],
            s_send.at[kind, b, step],
            s_recv.at[kind, b, step],
            blk,
            peer_of(step),
        )

    def s_local(kind, b):
        return pltpu.make_async_copy(
            sigma.at[kind, part(me, own), b],
            s_refs[kind].at[:, 0, b, part(me, rows), :],
            local_s.at[kind, b],
        )

    barrier = pltpu.get_barrier_semaphore()

    def greet(step):
        pl.semaphore_signal(barrier, inc=1, device_id=(blk, peer_of(step)), device_id_type=MESH)

    each(greet)

    @pl.when(has_left)
    def _():
        pl.semaphore_signal(barrier, inc=1, device_id=(blk - 1, me), device_id_type=MESH)

    @pl.when(has_right)
    def _():
        pl.semaphore_signal(barrier, inc=1, device_id=(blk + 1, me), device_id_type=MESH)

    for b in range(blocks):
        for kind in range(2):
            g_local(kind, b).start()
    v_mine = pltpu.make_async_copy(v_ref, v_all.at[1], local_v.at[0])
    v_mine.start()

    pl.semaphore_wait(barrier, n_eng - 1 + has_left.astype(jnp.int32) + has_right.astype(jnp.int32))

    for b in range(blocks):
        for kind in range(2):
            each(lambda step: g_copy(kind, b, step).start())

    @pl.when(has_left)
    def _():
        v_copy(0).start()

    @pl.when(has_right)
    def _():
        v_copy(1).start()

    @pl.when(jnp.logical_not(has_left))
    def _():
        polar[0] = jnp.zeros(polar.shape[1:], polar.dtype)
        v_all[0] = jnp.zeros(v_all.shape[1:], v_all.dtype)

    @pl.when(jnp.logical_not(has_right))
    def _():
        polar[2] = jnp.zeros(polar.shape[1:], polar.dtype)
        v_all[2] = jnp.zeros(v_all.shape[1:], v_all.dtype)

    lane_tiles = size // LANES
    tiles = (rows // PACK) * lane_tiles
    half = PACK // 2

    def tile_of(tile):
        row, lane = lax.div(tile, lane_tiles), lax.rem(tile, lane_tiles)
        return part(row, PACK), part(lane, LANES)

    for b in range(blocks):
        for kind in range(2):
            g_local(kind, b).wait()
            each(lambda step: g_copy(kind, b, step).wait_recv())

        def polar_tile(tile):
            at = tile_of(tile)
            lesser = green[0, :, b, at[0], at[1]]
            greater = green[1, :, b, at[0], at[1]]
            out = []
            for top in (0, half):
                first = lesser.astype(jnp.float32)[:, top : top + half]
                second = greater.astype(jnp.float32)[:, top : top + half] * scale
                out.append(correlate(first, second))
            polar_el[:, b, at[0], at[1]] = jnp.concatenate(out, axis=1).astype(jnp.bfloat16)

        each(polar_tile, 0, tiles)

        def send_slot(slot):
            each(lambda step: p_copy(slot, b, step).start())
            p_local(slot, b).start()

        each(send_slot, 0, own)

    v_mine.wait()

    @pl.when(has_left)
    def _():
        v_copy(0).wait_send()
        v_copy(1).wait_recv()

    @pl.when(has_right)
    def _():
        v_copy(1).wait_send()
        v_copy(0).wait_recv()

    def screen_slot(slot):
        diag_minus, up_minus = polar[0, slot, 0], polar[0, slot, 1]
        diag_zero, up_zero = polar[1, slot, 0], polar[1, slot, 1]
        diag_plus, up_plus = polar[2, slot, 0], polar[2, slot, 1]
        q_minus = dot(v_all[0, 2], diag_minus) + dot_t(v_all[1, 0], up_minus)
        q_zero = (
            dot(v_all[0, 2], up_minus)
            + dot(v_all[1, 0], diag_zero)
            + dot_t(v_all[1, 1], up_zero)
        )
        q_plus = dot(v_all[1, 0], up_zero) + dot(v_all[1, 1], diag_plus)
        q_far = dot(v_all[1, 1], up_plus).astype(jnp.bfloat16)
        q_minus = q_minus.astype(jnp.bfloat16)
        q_zero = q_zero.astype(jnp.bfloat16)
        q_plus = q_plus.astype(jnp.bfloat16)
        w_diag = dot(q_minus, v_all[0, 1]) + dot(q_zero, v_all[1, 0]) + dot(q_plus, v_all[1, 2])
        w_upper = dot(q_zero, v_all[1, 1]) + dot(q_plus, v_all[2, 0]) + dot(q_far, v_all[2, 2])
        w_own[slot, 0] = w_diag.astype(jnp.bfloat16)
        w_own[slot, 1] = w_upper.astype(jnp.bfloat16)

    def screen_step(step):
        @pl.when(step < own)
        def _():
            for b in range(blocks):
                p_local(step, b).wait()
                each(lambda other: p_copy(step, b, other).wait_recv())

            @pl.when(has_left)
            def _():
                halo_copy(step, 0).start()

            @pl.when(has_right)
            def _():
                halo_copy(step, 1).start()

        @pl.when(step > 0)
        def _():
            slot = step - 1

            @pl.when(has_left)
            def _():
                halo_copy(slot, 1).wait_recv()

            @pl.when(has_right)
            def _():
                halo_copy(slot, 0).wait_recv()

            screen_slot(slot)
            each(lambda other: w_copy(slot, other).start())
            w_local(slot).start()

    each(screen_step, 0, own + 1)

    def take_slot(slot):
        w_local(slot).wait()
        each(lambda other: w_copy(slot, other).wait_recv())

    each(take_slot, 0, own)

    for b in range(blocks):

        def sigma_tile(tile):
            at = tile_of(tile)
            screened = w_el[:, b, at[0], at[1]]
            for kind, combine in ((0, convolve), (1, correlate)):
                values = green[kind, :, b, at[0], at[1]]
                out = []
                for top in (0, half):
                    first = values.astype(jnp.float32)[:, top : top + half]
                    second = screened.astype(jnp.float32)[:, top : top + half] * weight_ref[kind]
                    out.append(combine(first, second))
                sigma[kind, :, b, at[0], at[1]] = jnp.concatenate(out, axis=1).astype(jnp.bfloat16)

        each(sigma_tile, 0, tiles)
        for kind in range(2):
            each(lambda step: s_copy(kind, b, step).start())
            s_local(kind, b).start()

    for b in range(blocks):
        for kind in range(2):
            each(lambda step: g_copy(kind, b, step).wait_send())

        def sent_slot(slot):
            each(lambda step: p_copy(slot, b, step).wait_send())

        each(sent_slot, 0, own)

    def sent_rest(slot):
        each(lambda step: w_copy(slot, step).wait_send())

        @pl.when(has_left)
        def _():
            halo_copy(slot, 0).wait_send()

        @pl.when(has_right)
        def _():
            halo_copy(slot, 1).wait_send()

    each(sent_rest, 0, own)
    for b in range(blocks):
        for kind in range(2):
            s_local(kind, b).wait()
            each(lambda step: s_copy(kind, b, step).wait())


def on_device(n_blk, n_eng, g_lesser, g_greater, coulomb, coupling, lag_slots):
    own, row_count, blocks, size = g_lesser.shape[:4]
    energies = own * n_eng
    rows = size // n_eng
    row_ids = lax.axis_index("blk") * row_count + jnp.arange(row_count, dtype=jnp.int32)
    kept_links = (coupling * (row_ids < row_count * n_blk - 1).astype(jnp.int32)).astype(jnp.bfloat16)
    upper = coulomb[0, 1] * kept_links[0]
    v_both = jnp.stack([coulomb[0, 0], upper, upper.T])
    slot_ids = jnp.arange(energies, dtype=jnp.int32)
    hits = jnp.sum((lag_slots[:, None] == slot_ids[None, :]).astype(jnp.float32), axis=0)
    mirrored = jnp.sum(
        (lag_slots[:, None] == ((energies - slot_ids) % energies)[None, :]).astype(jnp.float32), axis=0
    )
    weights = jnp.stack([hits, mirrored]) * energies ** (-0.5)
    weights = jnp.broadcast_to(weights[:, :, None, None], (2, energies, PACK // 2, LANES))
    dma, bf16 = pltpu.SemaphoreType.DMA, jnp.bfloat16
    element = (energies, blocks, rows, size)
    any_space = pl.BlockSpec(memory_space=pl.ANY)
    vmem = pl.BlockSpec(memory_space=pltpu.VMEM)
    out = jax.ShapeDtypeStruct(g_lesser.shape, bf16)
    return pl.pallas_call(
        functools.partial(kernel, n_blk, n_eng),
        out_shape=(out, out),
        in_specs=[any_space, any_space, vmem, vmem],
        out_specs=(any_space, any_space),
        scratch_shapes=[
            pltpu.VMEM((2, *element), bf16),
            pltpu.VMEM(element, bf16),
            pltpu.VMEM((3, own, blocks, size, size), bf16),
            pltpu.VMEM((3, 3, size, size), bf16),
            pltpu.VMEM((own, blocks, size, size), bf16),
            pltpu.VMEM(element, bf16),
            pltpu.VMEM((2, *element), bf16),
            dma((2, blocks, n_eng)),
            dma((2, blocks, n_eng)),
            dma((own, blocks, n_eng)),
            dma((own, blocks, n_eng)),
            dma((own, 2)),
            dma((own, 2)),
            dma((2,)),
            dma((2,)),
            dma((own, n_eng)),
            dma((own, n_eng)),
            dma((2, blocks, n_eng)),
            dma((2, blocks, n_eng)),
            dma((2, blocks)),
            dma((own, blocks)),
            dma((own,)),
            dma((2, blocks)),
            dma((1,)),
        ],
        compiler_params=pltpu.CompilerParams(
            collective_id=0, has_side_effects=True, vmem_limit_bytes=40 * 1024 * 1024
        ),
    )(g_lesser, g_greater, v_both, weights)


def solution(mesh):
    n_blk, n_eng = mesh.shape["blk"], mesh.shape["eng"]
    return jax.shard_map(
        functools.partial(on_device, n_blk, n_eng),
        mesh=mesh,
        in_specs=(
            P("eng", "blk", None, None, None),
            P("eng", "blk", None, None, None),
            P("blk", None, None, None),
            P("blk"),
            P(),
        ),
        out_specs=(P("eng", "blk", None, None, None), P("eng", "blk", None, None, None)),
        check_vma=False,
    )
```

```python
import functools

import jax
import jax.numpy as jnp
from jax import lax
from jax.experimental import pallas as pl
from jax.experimental.pallas import tpu as pltpu
from jax.sharding import PartitionSpec as P

MESH = pl.DeviceIdType.MESH
LANES = 128
PACK = 16
DIRECT = 8


def correlate(first, second, sign=1.0):
    count = first.shape[0]
    if sign > 0 and count > DIRECT and count % 2 == 0:
        half = count // 2
        first_lo, first_hi = first[:half], first[half:]
        second_lo, second_hi = second[:half] * 0.5, second[half:] * 0.5
        even = correlate(first_lo + first_hi, second_lo + second_hi)
        odd = correlate(first_lo - first_hi, second_lo - second_hi, -1.0)
        return jnp.concatenate([even + odd, even - odd], axis=0)
    wrapped = jnp.concatenate([first, first if sign > 0 else -first], axis=0)
    total = second[0:1] * wrapped[:count]
    for j in range(1, count):
        total = total + second[j : j + 1] * wrapped[j : j + count]
    return total


def convolve(first, second, sign=1.0):
    count = first.shape[0]
    if sign > 0 and count > DIRECT and count % 2 == 0:
        half = count // 2
        first_lo, first_hi = first[:half], first[half:]
        second_lo, second_hi = second[:half] * 0.5, second[half:] * 0.5
        even = convolve(first_lo + first_hi, second_lo + second_hi)
        odd = convolve(first_lo - first_hi, second_lo - second_hi, -1.0)
        return jnp.concatenate([even + odd, even - odd], axis=0)
    wrapped = jnp.concatenate([first if sign > 0 else -first, first], axis=0)
    total = second[0:1] * wrapped[count:]
    for j in range(1, count):
        total = total + second[j : j + 1] * wrapped[count - j : 2 * count - j]
    return total


def dot(left, right):
    return jnp.dot(left, right, preferred_element_type=jnp.float32)


def dot_t(left, right):
    return lax.dot_general(
        left, right, (((1,), (1,)), ((), ())), preferred_element_type=jnp.float32
    )


def kernel(
    n_blk,
    n_eng,
    gl_ref,
    gg_ref,
    v_ref,
    weight_ref,
    sl_ref,
    sg_ref,
    green,
    polar_el,
    polar,
    v_all,
    w_own,
    w_el,
    sigma,
    g_send,
    g_recv,
    p_send,
    p_recv,
    halo_send,
    halo_recv,
    v_send,
    v_recv,
    w_send,
    w_recv,
    s_send,
    s_recv,
    local_g,
    local_p,
    local_w,
    local_s,
    local_v,
):
    blk = lax.axis_index("blk")
    me = lax.axis_index("eng")
    own, blocks, size = gl_ref.shape[0], gl_ref.shape[2], gl_ref.shape[3]
    energies = own * n_eng
    rows = size // n_eng
    scale = energies ** (-0.5)
    has_left, has_right = blk > 0, blk < n_blk - 1
    g_refs, s_refs = (gl_ref, gg_ref), (sl_ref, sg_ref)

    def peer_of(step):
        return lax.rem(me + step, n_eng)

    def part(index, length):
        return pl.ds(pl.multiple_of(index * length, length), length)

    def remote(src, dst, send, recv, blk_to, eng_to):
        return pltpu.make_async_remote_copy(
            src_ref=src,
            dst_ref=dst,
            send_sem=send,
            recv_sem=recv,
            device_id=(blk_to, eng_to),
            device_id_type=MESH,
        )

    def each(body, low=1, high=n_eng):
        def run(step, carry):
            body(step)
            return carry

        lax.fori_loop(low, high, run, 0)

    def g_copy(kind, b, step):
        return remote(
            g_refs[kind].at[:, 0, b, part(peer_of(step), rows), :],
            green.at[kind, part(me, own), b],
            g_send.at[kind, b, step],
            g_recv.at[kind, b, step],
            blk,
            peer_of(step),
        )

    def g_local(kind, b):
        return pltpu.make_async_copy(
            g_refs[kind].at[:, 0, b, part(me, rows), :],
            green.at[kind, part(me, own), b],
            local_g.at[kind, b],
        )

    def p_copy(slot, b, step):
        return remote(
            polar_el.at[peer_of(step) * own + slot, b],
            polar.at[1, slot, b, part(me, rows), :],
            p_send.at[slot, b, step],
            p_recv.at[slot, b, step],
            blk,
            peer_of(step),
        )

    def p_local(slot, b):
        return pltpu.make_async_copy(
            polar_el.at[me * own + slot, b],
            polar.at[1, slot, b, part(me, rows), :],
            local_p.at[slot, b],
        )

    def halo_copy(slot, side, b):
        return remote(
            polar.at[1, slot, b],
            polar.at[2 - 2 * side, slot, b],
            halo_send.at[slot, side, b],
            halo_recv.at[slot, side, b],
            lax.rem(blk - 1 + 2 * side + n_blk, n_blk),
            me,
        )

    def v_copy(side):
        return remote(
            v_ref,
            v_all.at[2 - 2 * side],
            v_send.at[side],
            v_recv.at[side],
            lax.rem(blk - 1 + 2 * side + n_blk, n_blk),
            me,
        )

    def w_copy(slot, step):
        return remote(
            w_own.at[slot, :, part(peer_of(step), rows), :],
            w_el.at[me * own + slot],
            w_send.at[slot, step],
            w_recv.at[slot, step],
            blk,
            peer_of(step),
        )

    def w_local(slot):
        return pltpu.make_async_copy(
            w_own.at[slot, :, part(me, rows), :], w_el.at[me * own + slot], local_w.at[slot]
        )

    def s_copy(kind, b, step):
        return remote(
            sigma.at[kind, part(peer_of(step), own), b],
            s_refs[kind].at[:, 0, b, part(me, rows), :],
            s_send.at[kind, b, step],
            s_recv.at[kind, b, step],
            blk,
            peer_of(step),
        )

    def s_local(kind, b):
        return pltpu.make_async_copy(
            sigma.at[kind, part(me, own), b],
            s_refs[kind].at[:, 0, b, part(me, rows), :],
            local_s.at[kind, b],
        )

    barrier = pltpu.get_barrier_semaphore()

    def greet(step):
        pl.semaphore_signal(barrier, inc=1, device_id=(blk, peer_of(step)), device_id_type=MESH)

    each(greet)

    @pl.when(has_left)
    def _():
        pl.semaphore_signal(barrier, inc=1, device_id=(blk - 1, me), device_id_type=MESH)

    @pl.when(has_right)
    def _():
        pl.semaphore_signal(barrier, inc=1, device_id=(blk + 1, me), device_id_type=MESH)

    for b in range(blocks):
        for kind in range(2):
            g_local(kind, b).start()
    v_mine = pltpu.make_async_copy(v_ref, v_all.at[1], local_v.at[0])
    v_mine.start()

    pl.semaphore_wait(barrier, n_eng - 1 + has_left.astype(jnp.int32) + has_right.astype(jnp.int32))

    for b in range(blocks):
        for kind in range(2):
            each(lambda step: g_copy(kind, b, step).start())

    @pl.when(has_left)
    def _():
        v_copy(0).start()

    @pl.when(has_right)
    def _():
        v_copy(1).start()

    @pl.when(jnp.logical_not(has_left))
    def _():
        polar[0] = jnp.zeros(polar.shape[1:], polar.dtype)
        v_all[0] = jnp.zeros(v_all.shape[1:], v_all.dtype)

    @pl.when(jnp.logical_not(has_right))
    def _():
        polar[2] = jnp.zeros(polar.shape[1:], polar.dtype)
        v_all[2] = jnp.zeros(v_all.shape[1:], v_all.dtype)

    lane_tiles = size // LANES
    tiles = (rows // PACK) * lane_tiles
    half = PACK // 2

    def tile_of(tile):
        row, lane = lax.div(tile, lane_tiles), lax.rem(tile, lane_tiles)
        return part(row, PACK), part(lane, LANES)

    for b in range(blocks):
        for kind in range(2):
            g_local(kind, b).wait()
            each(lambda step: g_copy(kind, b, step).wait_recv())

        def polar_tile(tile):
            at = tile_of(tile)
            lesser = green[0, :, b, at[0], at[1]]
            greater = green[1, :, b, at[0], at[1]]
            out = []
            for top in (0, half):
                first = lesser.astype(jnp.float32)[:, top : top + half]
                second = greater.astype(jnp.float32)[:, top : top + half] * scale
                out.append(correlate(first, second))
            polar_el[:, b, at[0], at[1]] = jnp.concatenate(out, axis=1).astype(jnp.bfloat16)

        each(polar_tile, 0, tiles)

        def send_slot(slot):
            each(lambda step: p_copy(slot, b, step).start())
            p_local(slot, b).start()

        each(send_slot, 0, own)

    v_mine.wait()

    @pl.when(has_left)
    def _():
        v_copy(0).wait_send()
        v_copy(1).wait_recv()

    @pl.when(has_right)
    def _():
        v_copy(1).wait_send()
        v_copy(0).wait_recv()

    def screen_slot(slot):
        diag_minus, up_minus = polar[0, slot, 0], polar[0, slot, 1]
        diag_zero, up_zero = polar[1, slot, 0], polar[1, slot, 1]
        diag_plus, up_plus = polar[2, slot, 0], polar[2, slot, 1]
        q_minus = dot(v_all[0, 2], diag_minus) + dot_t(v_all[1, 0], up_minus)
        q_zero = (
            dot(v_all[0, 2], up_minus)
            + dot(v_all[1, 0], diag_zero)
            + dot_t(v_all[1, 1], up_zero)
        )
        q_plus = dot(v_all[1, 0], up_zero) + dot(v_all[1, 1], diag_plus)
        q_far = dot(v_all[1, 1], up_plus).astype(jnp.bfloat16)
        q_minus = q_minus.astype(jnp.bfloat16)
        q_zero = q_zero.astype(jnp.bfloat16)
        q_plus = q_plus.astype(jnp.bfloat16)
        w_diag = dot(q_minus, v_all[0, 1]) + dot(q_zero, v_all[1, 0]) + dot(q_plus, v_all[1, 2])
        w_upper = dot(q_zero, v_all[1, 1]) + dot(q_plus, v_all[2, 0]) + dot(q_far, v_all[2, 2])
        w_own[slot, 0] = w_diag.astype(jnp.bfloat16)
        w_own[slot, 1] = w_upper.astype(jnp.bfloat16)

    def pass_on(slot, b):
        p_local(slot, b).wait()
        each(lambda other: p_copy(slot, b, other).wait_recv())

        @pl.when(has_left)
        def _():
            halo_copy(slot, 0, b).start()

        @pl.when(has_right)
        def _():
            halo_copy(slot, 1, b).start()

    for b in range(blocks - 1):
        each(lambda slot: pass_on(slot, b), 0, own)

    def screen_step(step):
        @pl.when(step < own)
        def _():
            pass_on(step, blocks - 1)

        @pl.when(step > 0)
        def _():
            slot = step - 1

            @pl.when(has_left)
            def _():
                for b in range(blocks):
                    halo_copy(slot, 1, b).wait_recv()

            @pl.when(has_right)
            def _():
                for b in range(blocks):
                    halo_copy(slot, 0, b).wait_recv()

            screen_slot(slot)
            each(lambda other: w_copy(slot, other).start())
            w_local(slot).start()

    each(screen_step, 0, own + 1)

    def take_slot(slot):
        w_local(slot).wait()
        each(lambda other: w_copy(slot, other).wait_recv())

    each(take_slot, 0, own)

    for b in range(blocks):
        for kind, combine in ((0, convolve), (1, correlate)):

            def sigma_tile(tile):
                at = tile_of(tile)
                screened = w_el[:, b, at[0], at[1]]
                values = green[kind, :, b, at[0], at[1]]
                out = []
                for top in (0, half):
                    first = values.astype(jnp.float32)[:, top : top + half]
                    second = screened.astype(jnp.float32)[:, top : top + half] * weight_ref[kind]
                    out.append(combine(first, second))
                sigma[kind, :, b, at[0], at[1]] = jnp.concatenate(out, axis=1).astype(jnp.bfloat16)

            each(sigma_tile, 0, tiles)
            each(lambda step: s_copy(kind, b, step).start())
            s_local(kind, b).start()

    for b in range(blocks):
        for kind in range(2):
            each(lambda step: g_copy(kind, b, step).wait_send())

        def sent_slot(slot):
            each(lambda step: p_copy(slot, b, step).wait_send())

        each(sent_slot, 0, own)

    def sent_rest(slot):
        each(lambda step: w_copy(slot, step).wait_send())

        @pl.when(has_left)
        def _():
            for b in range(blocks):
                halo_copy(slot, 0, b).wait_send()

        @pl.when(has_right)
        def _():
            for b in range(blocks):
                halo_copy(slot, 1, b).wait_send()

    each(sent_rest, 0, own)
    for b in range(blocks):
        for kind in range(2):
            s_local(kind, b).wait()
            each(lambda step: s_copy(kind, b, step).wait())


def on_device(n_blk, n_eng, g_lesser, g_greater, coulomb, coupling, lag_slots):
    own, row_count, blocks, size = g_lesser.shape[:4]
    energies = own * n_eng
    rows = size // n_eng
    row_ids = lax.axis_index("blk") * row_count + jnp.arange(row_count, dtype=jnp.int32)
    kept_links = (coupling * (row_ids < row_count * n_blk - 1).astype(jnp.int32)).astype(jnp.bfloat16)
    upper = coulomb[0, 1] * kept_links[0]
    v_both = jnp.stack([coulomb[0, 0], upper, upper.T])
    slot_ids = jnp.arange(energies, dtype=jnp.int32)
    hits = jnp.sum((lag_slots[:, None] == slot_ids[None, :]).astype(jnp.float32), axis=0)
    mirrored = jnp.sum(
        (lag_slots[:, None] == ((energies - slot_ids) % energies)[None, :]).astype(jnp.float32), axis=0
    )
    weights = jnp.stack([hits, mirrored]) * energies ** (-0.5)
    weights = jnp.broadcast_to(weights[:, :, None, None], (2, energies, PACK // 2, LANES))
    dma, bf16 = pltpu.SemaphoreType.DMA, jnp.bfloat16
    element = (energies, blocks, rows, size)
    any_space = pl.BlockSpec(memory_space=pl.ANY)
    vmem = pl.BlockSpec(memory_space=pltpu.VMEM)
    out = jax.ShapeDtypeStruct(g_lesser.shape, bf16)
    return pl.pallas_call(
        functools.partial(kernel, n_blk, n_eng),
        out_shape=(out, out),
        in_specs=[any_space, any_space, vmem, vmem],
        out_specs=(any_space, any_space),
        scratch_shapes=[
            pltpu.VMEM((2, *element), bf16),
            pltpu.VMEM(element, bf16),
            pltpu.VMEM((3, own, blocks, size, size), bf16),
            pltpu.VMEM((3, 3, size, size), bf16),
            pltpu.VMEM((own, blocks, size, size), bf16),
            pltpu.VMEM(element, bf16),
            pltpu.VMEM((2, *element), bf16),
            dma((2, blocks, n_eng)),
            dma((2, blocks, n_eng)),
            dma((own, blocks, n_eng)),
            dma((own, blocks, n_eng)),
            dma((own, 2, blocks)),
            dma((own, 2, blocks)),
            dma((2,)),
            dma((2,)),
            dma((own, n_eng)),
            dma((own, n_eng)),
            dma((2, blocks, n_eng)),
            dma((2, blocks, n_eng)),
            dma((2, blocks)),
            dma((own, blocks)),
            dma((own,)),
            dma((2, blocks)),
            dma((1,)),
        ],
        compiler_params=pltpu.CompilerParams(
            collective_id=0, has_side_effects=True, vmem_limit_bytes=40 * 1024 * 1024
        ),
    )(g_lesser, g_greater, v_both, weights)


def solution(mesh):
    n_blk, n_eng = mesh.shape["blk"], mesh.shape["eng"]
    return jax.shard_map(
        functools.partial(on_device, n_blk, n_eng),
        mesh=mesh,
        in_specs=(
            P("eng", "blk", None, None, None),
            P("eng", "blk", None, None, None),
            P("blk", None, None, None),
            P("blk"),
            P(),
        ),
        out_specs=(P("eng", "blk", None, None, None), P("eng", "blk", None, None, None)),
        check_vma=False,
    )
```
